512 devices in a mesh: row: 32 (over y, z_lo), col: 16 (over z_hi, x, core).
Axes of the slice: x: 4, y: 8, z: 8 (z_hi: 2, z_lo: 4; z = z_hi * 4 + z_lo), core: 2. Of those that a mesh axis runs over, the one named last changes fastest.
Arguments:
- signal: bfloat16 [8, 1024, 2048], P(None, 'row', 'col'), may hold values from -6 to 6
- filter_real: bfloat16 [8, 1024, 2048], P(None, 'row', 'col'), may hold values from -6 to 6
- filter_imag: bfloat16 [8, 1024, 2048], P(None, 'row', 'col'), may hold values from -6 to 6
- skip: float32 [8], replicated, may hold values from 0.5 to 1.5
Outputs:
- output: bfloat16 [8, 1024, 2048], P(None, 'row', 'col')
The draws below stay inside these ranges and needn't reach their ends.
All inputs are finite; a program needn't handle non-finite values.
Results may differ from the reference program's by a relative error of at most 0.0064.
Values may be sent and summed in bfloat16 or wider, within the bound.
A program may use at most 64 MiB of HBM per device.

```python
import math
import jax
import jax.numpy as jnp
from jax import lax

CHANNELS = 8
N1 = 1024
N2 = 2048


def levels(rng, shape, cuts, smallest, largest):
    level, own = 1.0, jax.random.fold_in(rng, 6)
    for axis_at, blocks in cuts:
        draws = jnp.exp(jax.random.uniform(jax.random.fold_in(own, axis_at), (blocks,), jnp.float32, smallest / len(cuts), largest / len(cuts)))
        level = level * jnp.repeat(draws, shape[axis_at] // blocks).reshape([-1 if axis == axis_at else 1 for axis in range(len(shape))])
    return level


def normal_values(own_key, dims, scale, most, cuts=(), kind=jnp.bfloat16):
    entries = jax.random.normal(own_key, dims, jnp.float32) * scale
    if len(cuts) > 0:
        entries = levels(own_key, dims, cuts, -0.22, 0.18) * entries
    return jnp.clip(entries, min=-most, max=most).astype(kind)


def setup_inputs(seed: int = 0) -> dict:
    key_list = jax.random.split(jax.random.key(seed), 5)
    signal = normal_values(key_list[0], (CHANNELS, N1, N2), 1.0, 6.0, ((1, 32), (2, 16)))
    filter_real = normal_values(key_list[1], (CHANNELS, N1, N2), 1.0, 6.0, ((1, 32), (2, 16)))
    filter_imag = normal_values(key_list[2], (CHANNELS, N1, N2), 1.0, 6.0, ((1, 32), (2, 16)))
    skip = jnp.clip(jax.random.uniform(key_list[3], (CHANNELS,), jnp.float32, 0.5, 1.5), 0.5, 1.5)
    return dict(signal=signal, filter_real=filter_real, filter_imag=filter_imag, skip=skip)


def phase_table(left_ids, right_ids, modulus):
    product = (left_ids[:, None] * right_ids[None, :]) % modulus
    angle = (-2.0 * math.pi / modulus) * product.astype(jnp.float32)
    return jnp.cos(angle), jnp.sin(angle)


def rounded(matrix):
    return lax.optimization_barrier(matrix.astype(jnp.bfloat16)).astype(jnp.float32)


def matmul(left, right):
    return jnp.dot(left, right, preferred_element_type=jnp.float32, precision=lax.Precision.HIGHEST)


def reference(signal, filter_real, filter_imag, skip):
    first_len = signal.shape[1]
    second_len = signal.shape[2]
    seq_len = first_len * second_len
    row_ids = jnp.arange(first_len, dtype=jnp.int32)
    col_ids = jnp.arange(second_len, dtype=jnp.int32)
    first_re, first_im = phase_table(row_ids, row_ids, first_len)
    first_re = rounded(first_re)
    first_im = rounded(first_im)
    second_re, second_im = phase_table(col_ids, col_ids, second_len)
    second_re = rounded(second_re)
    second_im = rounded(second_im)
    twist_re, twist_im = phase_table(row_ids, col_ids, seq_len)

    def one_channel(members):
        series = members[0].astype(jnp.float32)
        filt_re = members[1].astype(jnp.float32)
        filt_im = members[2].astype(jnp.float32)
        col_re = matmul(first_re, series)
        col_im = matmul(first_im, series)
        mixed_re = rounded(col_re * twist_re - col_im * twist_im)
        mixed_im = rounded(col_re * twist_im + col_im * twist_re)
        spec_re = matmul(mixed_re, second_re) - matmul(mixed_im, second_im)
        spec_im = matmul(mixed_re, second_im) + matmul(mixed_im, second_re)
        prod_re = rounded(spec_re * filt_re - spec_im * filt_im)
        prod_im = rounded(spec_re * filt_im + spec_im * filt_re)
        back_re = matmul(prod_re, second_re) + matmul(prod_im, second_im)
        back_im = matmul(prod_im, second_re) - matmul(prod_re, second_im)
        unwound_re = rounded(back_re * twist_re + back_im * twist_im)
        unwound_im = rounded(back_im * twist_re - back_re * twist_im)
        total = matmul(first_re, unwound_re) + matmul(first_im, unwound_im)
        return (total / seq_len + members[3] * series).astype(jnp.bfloat16)

    return lax.map(one_channel, (signal, filter_real, filter_imag, skip))
```

```python
import functools

import jax
import jax.numpy as jnp
import numpy as np
from jax import lax
from jax.experimental import pallas as pl
from jax.experimental.pallas import tpu as pltpu
from jax.sharding import PartitionSpec as P

MESH = pl.DeviceIdType.MESH
F32, BF16 = jnp.float32, jnp.bfloat16
N1, N2 = 1024, 2048
SEQ = N1 * N2


def unit(product, modulus):
    angle = 2.0 * np.pi / modulus * (product % modulus)
    return np.cos(angle), np.sin(angle)


def tables():
    g = lambda *dims: np.meshgrid(*[np.arange(n) for n in dims], indexing="ij")
    bl, ka, dl, dh, kb, r, i = g(4, 4, 8, 2, 4, 32, 8)
    k1 = 16 * (8 * bl + dl + 32 * dh) + 4 * ka + kb
    c, s = unit(k1 * (32 * r + i), N1)
    first = np.stack([c, -s], axis=1).reshape(4, 512, 256)
    ka, dl, dh, kb, k, j = g(4, 8, 2, 4, 4, 32)
    c, s = unit((16 * (dl + 32 * dh) + 4 * ka + kb) * 8 * k, N1)
    turn = np.stack([c, -s]).reshape(2, 4, 64, 128)
    c, s = unit(np.outer(np.arange(64), np.arange(64)), 64)
    wide = np.einsum("pqks,bc->pbksqc", np.array([[c, s], [-s, c]]), np.eye(4)).reshape(512, 512)
    ks, ka, j = g(64, 4, 32)
    c, s = unit(j * ks, N2)
    bend = np.stack([c, -s]).reshape(2, 64, 128)
    j, kj0, q = g(32, 2, 16)
    c, s = unit(j * (2 * q + kj0), 32)
    short = np.einsum("pqjhx,ab->pajqhbx", np.array([[c, -s], [s, c]]), np.eye(4)).reshape(256, 256)
    half = lambda a: np.asarray(a, np.float32).astype(BF16)
    full = lambda a: np.asarray(a, np.float32)
    return (
        half(first),
        half(first.reshape(2048, 256).T),
        full(turn),
        half(wide),
        half(wide.T),
        full(bend),
        half(short),
        half(short.T),
    )


def far_first(step, size):
    half = (step + 1) >> 1
    return (size // 2 + jnp.where((step & 1) == 1, -half, half)) & (size - 1)


def kernel(
    signal, filt_re, filt_im, skip,
    c_first, c_back, c_turn, c_wide, c_wideb, c_bend, c_short, c_shortb,
    out,
    x_in, out1, in1, out2, in2, out3, in3, out4, in4, filt_in, filt_f, filt_h, twist, mixed,
    first, back, turn, wide, wideb, bend, short, shortb,
    load_sem, send_sem, recv_sem,
):
    row, col = lax.axis_index("row"), lax.axis_index("col")
    y, zl = row >> 2, row & 3
    z, xs, core = ((col >> 3) << 2) | zl, (col >> 1) & 3, col & 1
    col_id = 4 * col + zl
    freq_id = 8 * (col >> 1) + 2 * zl + core

    loads = [
        pltpu.make_async_copy(a, b, load_sem.at[n])
        for n, (a, b) in enumerate((
            (signal, x_in), (c_first, first), (c_turn, turn), (c_wide, wide), (c_bend, bend),
            (c_short, short), (c_shortb, shortb), (c_wideb, wideb), (c_back, back),
        ))
    ]
    for load in loads:
        load.start()

    def row_peer(u):
        r2 = (((y + far_first(u >> 2, 8)) & 7) << 2) | ((zl + 3 - (u & 3)) & 3)
        return r2, (r2, col)

    def plane_peer(u):
        z2 = (z + far_first(u >> 3, 8)) & 7
        x2 = (xs + far_first((u >> 1) & 3, 4)) & 3
        zl2, col2 = z2 & 3, ((z2 >> 2) << 3) | (x2 << 1) | (core ^ 1 ^ (u & 1))
        return 4 * col2 + zl2, 8 * (col2 >> 1) + 2 * zl2 + (col2 & 1), (4 * y + zl2, col2)

    own = (col >> 1) == y
    barrier = pltpu.get_barrier_semaphore()

    @pl.loop(0, 31)
    def _(u):
        pl.semaphore_signal(barrier, inc=1, device_id=row_peer(u)[1], device_id_type=MESH)

    @pl.loop(0, 63)
    def _(u):
        pl.semaphore_signal(barrier, inc=1, device_id=plane_peer(u)[2], device_id_type=MESH)

    @pl.loop(0, 16)
    def _(u):
        @pl.when(jnp.logical_not(own & (u == col)))
        def _():
            pl.semaphore_signal(
                barrier, inc=1, device_id=(4 * (col >> 1) + zl, u), device_id_type=MESH
            )

    lane = lax.broadcasted_iota(jnp.int32, (8, 128), 1)
    low64, low32 = lane < 64, (lane & 32) == 0
    low4 = lax.broadcasted_iota(jnp.int32, (8, 128), 0) < 4

    def regroup(a):
        u = [[None, None], [None, None]]
        for e in range(2):
            u[0][e] = jnp.where(low64, a[e], pltpu.roll(a[2 + e], 64, 2))
            u[1][e] = jnp.where(low64, pltpu.roll(a[e], 64, 2), a[2 + e])
        v = []
        for b in range(2):
            v.append(jnp.where(low32, u[b][0], pltpu.roll(u[b][1], 32, 2)))
            v.append(jnp.where(low32, pltpu.roll(u[b][0], 96, 2), u[b][1]))
        return v

    loads[0].wait()
    pieces = x_in[...].astype(F32)
    for b, piece in enumerate(regroup([pieces[:, 8 * k : 8 * k + 8, :] for k in range(4)])):
        out1[:, b] = piece.astype(BF16)
    in1[row] = out1[y, zl]

    pl.semaphore_wait(barrier, 31 + 63 + 16 - own.astype(jnp.int32))

    def send1(u):
        r2, device = row_peer(u)
        return pltpu.make_async_remote_copy(
            src_ref=out1.at[r2 >> 2, r2 & 3], dst_ref=in1.at[row],
            send_sem=send_sem.at[0], recv_sem=recv_sem.at[0], device_id=device, device_id_type=MESH,
        )

    @pl.loop(0, 31)
    def _(u):
        send1(u).start()

    @pl.loop(0, 16)
    def _(u):
        c = (y + far_first(u >> 1, 8)) & 7
        h = u & 1
        keep = own & (c == y) & (h == core)
        for n, part in enumerate((filt_re, filt_im)):
            source, target = part.at[c, pl.ds(16 * h, 16)], filt_in.at[n, col]

            @pl.when(keep)
            def _():
                pltpu.make_async_copy(source, target, recv_sem.at[4]).start()

            @pl.when(jnp.logical_not(keep))
            def _():
                pltpu.make_async_remote_copy(
                    src_ref=source, dst_ref=target, send_sem=send_sem.at[4], recv_sem=recv_sem.at[4],
                    device_id=(4 * c + zl, 2 * y + h), device_id_type=MESH,
                ).start()

    @pl.loop(0, 32)
    def _(dl):
        sub = lax.broadcasted_iota(jnp.int32, (8, 128), 0)
        k1 = 16 * (dl + 32 * (sub >> 2)) + 4 * (lane >> 5) + (sub & 3)
        n2 = 32 * col_id + (lane & 31)
        angle = (-2.0 * np.pi / SEQ) * (k1 * n2).astype(F32)
        twist[0, dl] = jnp.cos(angle)
        twist[1, dl] = jnp.sin(angle)

    def arrived(buffer, count, n):
        view = buffer.at[pl.ds(0, count)]
        pltpu.make_async_copy(view, view, recv_sem.at[n]).wait()

    for load in loads[1:]:
        load.wait()
    arrived(in1, 31, 0)

    columns = in1[...].astype(F32).reshape(256, 128).astype(BF16)
    for block in range(4):
        part = jnp.dot(first[block], columns, preferred_element_type=F32).reshape(2, 4, 8, 8, 128)
        turned = [[], []]
        for ka in range(4):
            t_re, t_im = turn[0, ka].reshape(8, 8, 128), turn[1, ka].reshape(8, 8, 128)
            turned[0].append(part[0, ka] * t_re - part[1, ka] * t_im)
            turned[1].append(part[0, ka] * t_im + part[1, ka] * t_re)
        summed = []
        for v in turned:
            u = [
                jnp.where(low64, v[e], v[2 + e]) + pltpu.roll(jnp.where(low64, v[2 + e], v[e]), 64, 2)
                for e in range(2)
            ]
            summed.append(
                jnp.where(low32, u[0] + pltpu.roll(u[0], 96, 2), u[1] + pltpu.roll(u[1], 32, 2))
            )
        at = pl.ds(8 * block, 8)
        w_re, w_im = twist[0, at], twist[1, at]
        m_re = summed[0] * w_re - summed[1] * w_im
        m_im = summed[0] * w_im + summed[1] * w_re
        out2[pl.ds(8 * block, 8)] = jnp.where(low4, m_re, pltpu.roll(m_im, 4, 1)).astype(BF16)
        out2[pl.ds(32 + 8 * block, 8)] = jnp.where(low4, pltpu.roll(m_re, 4, 1), m_im).astype(BF16)
    in2[col_id] = out2[freq_id]

    @pl.loop(0, 63)
    def _(u):
        _, d2, device = plane_peer(u)
        pltpu.make_async_remote_copy(
            src_ref=out2.at[d2], dst_ref=in2.at[col_id],
            send_sem=send_sem.at[1], recv_sem=recv_sem.at[1], device_id=device, device_id_type=MESH,
        ).start()

    for n in range(2):
        view = filt_in.at[n]
        if n == 0:
            pltpu.make_async_copy(filt_in, filt_in, recv_sem.at[4]).wait()
        filt_f[n] = filt_in[n].astype(F32).reshape(256, 128)
        for pair in range(2):
            rows = [
                filt_f[n, pl.ds(4 * ka + 2 * pair + e, 16, stride=16), :]
                for e in range(2)
                for ka in range(4)
            ]
            turned = jnp.concatenate(rows, axis=0).T
            upper, lower = turned[:64].reshape(8, 8, 128), turned[64:].reshape(8, 8, 128)
            filt_h[n, 2 * pair] = jnp.where(low64, upper, pltpu.roll(lower, 64, 2)).reshape(64, 128)
            filt_h[n, 2 * pair + 1] = jnp.where(low64, pltpu.roll(upper, 64, 2), lower).reshape(64, 128)

    arrived(in2, 63, 1)

    series = in2[...].astype(F32).reshape(512, 128).astype(BF16)
    part = jnp.dot(wide[...], series, preferred_element_type=F32).reshape(2, 4, 64, 128)
    b_re, b_im = bend[0], bend[1]
    bent = jnp.concatenate(
        [part[0] * b_re - part[1] * b_im, part[0] * b_im + part[1] * b_re], axis=2
    ).reshape(256, 256).astype(BF16)
    spec = jnp.dot(bent, short[...], preferred_element_type=F32)
    s_re, s_im = spec[:, :128], spec[:, 128:]
    h_re, h_im = filt_h[0].reshape(256, 128), filt_h[1].reshape(256, 128)
    prod = jnp.concatenate([s_re * h_re - s_im * h_im, s_re * h_im + s_im * h_re], axis=1).astype(BF16)
    part = jnp.dot(prod, shortb[...], preferred_element_type=F32).reshape(4, 64, 256)
    p_re, p_im = part[:, :, :128], part[:, :, 128:]
    bent = jnp.concatenate(
        [p_re * b_re + p_im * b_im, p_im * b_re - p_re * b_im], axis=0
    ).reshape(512, 128).astype(BF16)
    out3[...] = jnp.dot(wideb[...], bent, preferred_element_type=F32).reshape(64, 8, 128).astype(BF16)
    in3[freq_id] = out3[col_id]

    @pl.loop(0, 63)
    def _(u):
        s2, _, device = plane_peer(u)
        pltpu.make_async_remote_copy(
            src_ref=out3.at[s2], dst_ref=in3.at[freq_id],
            send_sem=send_sem.at[2], recv_sem=recv_sem.at[2], device_id=device, device_id_type=MESH,
        ).start()

    arrived(in3, 63, 2)

    for block in range(4):
        even = in3[pl.ds(8 * block, 8)].astype(F32)
        odd = in3[pl.ds(32 + 8 * block, 8)].astype(F32)
        e_re = jnp.where(low4, even, pltpu.roll(odd, 4, 1))
        e_im = jnp.where(low4, pltpu.roll(even, 4, 1), odd)
        at = pl.ds(8 * block, 8)
        w_re, w_im = twist[0, at], twist[1, at]
        spread = []
        for g in (e_re * w_re + e_im * w_im, e_im * w_re - e_re * w_im):
            u = [jnp.where(low32, g, pltpu.roll(g, 32, 2)), jnp.where(low32, pltpu.roll(g, 96, 2), g)]
            r = [pltpu.roll(a, 64, 2) for a in u]
            spread.append(
                [jnp.where(low64, u[e], r[e]) for e in range(2)]
                + [jnp.where(low64, r[e], u[e]) for e in range(2)]
            )
        for ka in range(4):
            t_re, t_im = turn[0, ka].reshape(8, 8, 128), turn[1, ka].reshape(8, 8, 128)
            g_re, g_im = spread[0][ka], spread[1][ka]
            mixed[block, 0, ka] = (g_re * t_re + g_im * t_im).reshape(64, 128).astype(BF16)
            mixed[block, 1, ka] = (g_im * t_re - g_re * t_im).reshape(64, 128).astype(BF16)
    total = jnp.dot(back[...], mixed[...].reshape(2048, 128), preferred_element_type=F32)
    result = total.reshape(32, 8, 128) * (1.0 / SEQ) + skip[y] * in1[...].astype(F32)
    out4[...] = result.astype(BF16)
    in4[row] = out4[row]

    @pl.loop(0, 31)
    def _(u):
        r2, device = row_peer(u)
        pltpu.make_async_remote_copy(
            src_ref=out4.at[r2], dst_ref=in4.at[row],
            send_sem=send_sem.at[3], recv_sem=recv_sem.at[3], device_id=device, device_id_type=MESH,
        ).start()

    def sent(buffer, count, n):
        view = buffer.at[pl.ds(0, count)]
        pltpu.make_async_copy(view, view, send_sem.at[n]).wait()

    sent(in1, 31, 0)
    sent(out2, 63, 1)
    sent(out3, 63, 2)

    @pl.when(own)
    def _():
        view = filt_in.at[:, pl.ds(0, 15)]
        pltpu.make_async_copy(view, view, send_sem.at[4]).wait()

    @pl.when(jnp.logical_not(own))
    def _():
        pltpu.make_async_copy(filt_in, filt_in, send_sem.at[4]).wait()

    arrived(in4, 31, 3)
    blocks = in4[...].astype(F32).reshape(8, 4, 8, 128)
    out[...] = jnp.concatenate(regroup([blocks[:, b] for b in range(4)]), axis=1).astype(BF16)
    sent(out4, 31, 3)


def solution(mesh):
    consts = tables()
    hbm, vmem = pl.BlockSpec(memory_space=pl.ANY), pl.BlockSpec(memory_space=pltpu.VMEM)
    like = lambda a, kind: pltpu.VMEM(a.shape, kind)
    kinds = (BF16, BF16, F32, BF16, BF16, F32, BF16, BF16)

    def local(signal, filter_real, filter_imag, skip):
        return pl.pallas_call(
            kernel,
            out_shape=jax.ShapeDtypeStruct(signal.shape, BF16),
            in_specs=[hbm] * 3 + [pl.BlockSpec(memory_space=pltpu.SMEM)] + [hbm] * 8,
            out_specs=vmem,
            scratch_shapes=[
                pltpu.VMEM((8, 32, 128), BF16),
                pltpu.VMEM((8, 4, 8, 128), BF16),
                pltpu.VMEM((32, 8, 128), BF16),
                pltpu.VMEM((64, 8, 128), BF16),
                pltpu.VMEM((64, 8, 128), BF16),
                pltpu.VMEM((64, 8, 128), BF16),
                pltpu.VMEM((64, 8, 128), BF16),
                pltpu.VMEM((32, 8, 128), BF16),
                pltpu.VMEM((32, 8, 128), BF16),
                pltpu.VMEM((2, 16, 16, 128), BF16),
                pltpu.VMEM((2, 256, 128), F32),
                pltpu.VMEM((2, 4, 64, 128), F32),
                pltpu.VMEM((2, 32, 8, 128), F32),
                pltpu.VMEM((4, 2, 4, 64, 128), BF16),
                *[like(a, kind) for a, kind in zip(consts, kinds)],
                pltpu.SemaphoreType.DMA((9,)),
                pltpu.SemaphoreType.DMA((5,)),
                pltpu.SemaphoreType.DMA((5,)),
            ],
            compiler_params=pltpu.CompilerParams(
                collective_id=0, has_side_effects=True, vmem_limit_bytes=56 << 20
            ),
        )(signal, filter_real, filter_imag, skip, *consts)

    block = P(None, "row", "col")
    return jax.shard_map(
        local, mesh=mesh, in_specs=(block, block, block, P()), out_specs=block, check_vma=False
    )
```

```python
import functools

import jax
import jax.numpy as jnp
import numpy as np
from jax import lax
from jax.experimental import pallas as pl
from jax.experimental.pallas import tpu as pltpu
from jax.sharding import PartitionSpec as P

MESH = pl.DeviceIdType.MESH
F32, BF16 = jnp.float32, jnp.bfloat16
N1, N2 = 1024, 2048
SEQ = N1 * N2


def unit(product, modulus):
    angle = 2.0 * np.pi / modulus * (product % modulus)
    return np.cos(angle), np.sin(angle)


def tables():
    g = lambda *dims: np.meshgrid(*[np.arange(n) for n in dims], indexing="ij")
    bl, ka, dl, dh, kb, r, i = g(4, 4, 8, 2, 4, 32, 8)
    k1 = 16 * (8 * bl + dl + 32 * dh) + 4 * ka + kb
    c, s = unit(k1 * (32 * r + i), N1)
    first = np.stack([c, -s], axis=1).reshape(4, 512, 256)
    ka, dl, dh, kb, k, j = g(4, 8, 2, 4, 4, 32)
    c, s = unit((16 * (dl + 32 * dh) + 4 * ka + kb) * 8 * k, N1)
    turn = np.stack([c, -s]).reshape(2, 4, 64, 128)
    c, s = unit(np.outer(np.arange(64), np.arange(64)), 64)
    wide = np.einsum("pqks,bc->pbksqc", np.array([[c, s], [-s, c]]), np.eye(4)).reshape(512, 512)
    ks, ka, j = g(64, 4, 32)
    c, s = unit(j * ks, N2)
    bend = np.stack([c, -s]).reshape(2, 64, 128)
    j, kj0, q = g(32, 2, 16)
    c, s = unit(j * (2 * q + kj0), 32)
    short = np.einsum("pqjhx,ab->pajqhbx", np.array([[c, -s], [s, c]]), np.eye(4)).reshape(256, 256)
    half = lambda a: np.asarray(a, np.float32).astype(BF16)
    full = lambda a: np.asarray(a, np.float32)
    return (
        half(first),
        half(first.reshape(2048, 256).T),
        full(turn),
        half(wide),
        half(wide.T.reshape(2, 4, 8, 8, 512).transpose(1, 0, 2, 3, 4).reshape(4, 128, 512)),
        full(bend),
        half(short),
        half(short.T),
    )


FAR8 = (4, 3, 5, 2, 6, 1, 7, 0)
FAR4 = (2, 1, 3, 0)


def kernel(
    signal, filt_re, filt_im, skip,
    c_first, c_back, c_turn, c_wide, c_wideb, c_bend, c_short, c_shortb,
    out,
    x_in, out1, in1, out2, in2, out3, in3, out4, in4, filt_in, filt_f, filt_h, twist, mixed,
    first, back, turn, wide, wideb, bend, short, shortb,
    load_sem, send_sem, recv_sem,
):
    row, col = lax.axis_index("row"), lax.axis_index("col")
    y, zl = row >> 2, row & 3
    z, xs, core = ((col >> 3) << 2) | zl, (col >> 1) & 3, col & 1
    col_id = 4 * col + zl
    freq_id = 8 * (col >> 1) + 2 * zl + core

    loads = [
        pltpu.make_async_copy(a, b, load_sem.at[n])
        for n, (a, b) in enumerate((
            (signal, x_in), (c_first, first), (c_turn, turn), (c_wide, wide), (c_bend, bend),
            (c_short, short), (c_shortb, shortb), (c_wideb, wideb), (c_back, back),
        ))
    ]
    for load in loads:
        load.start()

    row_peers = []
    for dy in FAR8:
        for dz in (3, 2, 1, 0):
            y2, zl2 = (y + dy) & 7, (zl + dz) & 3
            row_peers.append((y2, zl2, (4 * y2 + zl2, col)))
    planes = []
    for dx in FAR4:
        planes.append([])
        for dz in FAR8:
            for dc in (1, 0):
                z2, x2, core2 = (z + dz) & 7, (xs + dx) & 3, core ^ dc
                zl2, col2 = z2 & 3, ((z2 >> 2) << 3) | (x2 << 1) | core2
                planes[-1].append((x2, z2, core2, (4 * y + zl2, col2)))
    cols = []
    for dz in (1, 0):
        for dx in FAR4:
            for dc in (1, 0):
                cols.append((col ^ (8 * dz + dc)) & 9 | (((xs + dx) & 3) << 1))

    own = (col >> 1) == y
    barrier = pltpu.get_barrier_semaphore()
    hear = lambda device: pl.semaphore_signal(barrier, inc=1, device_id=device, device_id_type=MESH)
    for col2 in cols[:-1]:
        hear((4 * (col >> 1) + zl, col2))

    @pl.when(jnp.logical_not(own))
    def _():
        hear((4 * (col >> 1) + zl, col))

    for peer in row_peers[:-1]:
        hear(peer[-1])
    for peer in sum(planes, [])[:-1]:
        hear(peer[-1])

    lane = lax.broadcasted_iota(jnp.int32, (8, 128), 1)
    low64, low32 = lane < 64, (lane & 32) == 0
    low4 = lax.broadcasted_iota(jnp.int32, (8, 128), 0) < 4

    def regroup(a):
        u = [[None, None], [None, None]]
        for e in range(2):
            u[0][e] = jnp.where(low64, a[e], pltpu.roll(a[2 + e], 64, 2))
            u[1][e] = jnp.where(low64, pltpu.roll(a[e], 64, 2), a[2 + e])
        v = []
        for b in range(2):
            v.append(jnp.where(low32, u[b][0], pltpu.roll(u[b][1], 32, 2)))
            v.append(jnp.where(low32, pltpu.roll(u[b][0], 96, 2), u[b][1]))
        return v

    loads[0].wait()
    pieces = x_in[...].astype(F32)
    for b, piece in enumerate(regroup([pieces[:, 8 * k : 8 * k + 8, :] for k in range(4)])):
        out1[:, b] = piece.astype(BF16)
    in1[row] = out1[y, zl]

    pl.semaphore_wait(barrier, 31 + 63 + 16 - own.astype(jnp.int32))

    def send(source, target, n, device):
        pltpu.make_async_remote_copy(
            src_ref=source, dst_ref=target, send_sem=send_sem.at[n], recv_sem=recv_sem.at[n],
            device_id=device, device_id_type=MESH,
        ).start()

    for y2, zl2, device in row_peers[:-1]:
        send(out1.at[y2, zl2], in1.at[row], 0, device)

    for dy in FAR8:
        for dc in (1, 0):
            c, h = (y + dy) & 7, core ^ dc
            for n, part in enumerate((filt_re, filt_im)):
                source, target = part.at[c, pl.ds(16 * h, 16)], filt_in.at[n, col]
                if dy or dc:
                    send(source, target, 4, (4 * c + zl, 2 * y + h))
                    continue

                @pl.when(own)
                def _():
                    pltpu.make_async_copy(source, target, recv_sem.at[4]).start()

                @pl.when(jnp.logical_not(own))
                def _():
                    send(source, target, 4, (4 * c + zl, 2 * y + h))

    @pl.loop(0, 32)
    def _(dl):
        sub = lax.broadcasted_iota(jnp.int32, (8, 128), 0)
        k1 = 16 * (dl + 32 * (sub >> 2)) + 4 * (lane >> 5) + (sub & 3)
        n2 = 32 * col_id + (lane & 31)
        angle = (-2.0 * np.pi / SEQ) * (k1 * n2).astype(F32)
        twist[0, dl] = jnp.cos(angle)
        twist[1, dl] = jnp.sin(angle)

    def arrived(buffer, count, n):
        view = buffer.at[pl.ds(0, count)]
        pltpu.make_async_copy(view, view, recv_sem.at[n]).wait()

    for load in loads[1:]:
        load.wait()
    arrived(in1, 31, 0)

    columns = in1[...].astype(F32).reshape(256, 128).astype(BF16)
    for peers in planes:
        block = peers[0][0]
        part = jnp.dot(first[block], columns, preferred_element_type=F32).reshape(2, 4, 8, 8, 128)
        turned = [[], []]
        for ka in range(4):
            t_re, t_im = turn[0, ka].reshape(8, 8, 128), turn[1, ka].reshape(8, 8, 128)
            turned[0].append(part[0, ka] * t_re - part[1, ka] * t_im)
            turned[1].append(part[0, ka] * t_im + part[1, ka] * t_re)
        summed = []
        for v in turned:
            u = [
                jnp.where(low64, v[e], v[2 + e]) + pltpu.roll(jnp.where(low64, v[2 + e], v[e]), 64, 2)
                for e in range(2)
            ]
            summed.append(
                jnp.where(low32, u[0] + pltpu.roll(u[0], 96, 2), u[1] + pltpu.roll(u[1], 32, 2))
            )
        at = pl.ds(8 * block, 8)
        w_re, w_im = twist[0, at], twist[1, at]
        m_re = summed[0] * w_re - summed[1] * w_im
        m_im = summed[0] * w_im + summed[1] * w_re
        out2[pl.ds(8 * block, 8)] = jnp.where(low4, m_re, pltpu.roll(m_im, 4, 1)).astype(BF16)
        out2[pl.ds(32 + 8 * block, 8)] = jnp.where(low4, pltpu.roll(m_re, 4, 1), m_im).astype(BF16)
        for x2, z2, core2, device in peers:
            d2 = ((z2 >> 2) << 5) | (x2 << 3) | ((z2 & 3) << 1) | core2
            if peers is planes[-1] and device is peers[-1][-1]:
                in2[col_id] = out2[d2]
            else:
                send(out2.at[d2], in2.at[col_id], 1, device)

    for n in range(2):
        view = filt_in.at[n]
        if n == 0:
            pltpu.make_async_copy(filt_in, filt_in, recv_sem.at[4]).wait()
        filt_f[n] = filt_in[n].astype(F32).reshape(256, 128)
        for pair in range(2):
            rows = [
                filt_f[n, pl.ds(4 * ka + 2 * pair + e, 16, stride=16), :]
                for e in range(2)
                for ka in range(4)
            ]
            turned = jnp.concatenate(rows, axis=0).T
            upper, lower = turned[:64].reshape(8, 8, 128), turned[64:].reshape(8, 8, 128)
            filt_h[n, 2 * pair] = jnp.where(low64, upper, pltpu.roll(lower, 64, 2)).reshape(64, 128)
            filt_h[n, 2 * pair + 1] = jnp.where(low64, pltpu.roll(upper, 64, 2), lower).reshape(64, 128)

    arrived(in2, 63, 1)

    series = in2[...].astype(F32).reshape(512, 128).astype(BF16)
    part = jnp.dot(wide[...], series, preferred_element_type=F32).reshape(2, 4, 64, 128)
    b_re, b_im = bend[0], bend[1]
    bent = jnp.concatenate(
        [part[0] * b_re - part[1] * b_im, part[0] * b_im + part[1] * b_re], axis=2
    ).reshape(256, 256).astype(BF16)
    spec = jnp.dot(bent, short[...], preferred_element_type=F32)
    s_re, s_im = spec[:, :128], spec[:, 128:]
    h_re, h_im = filt_h[0].reshape(256, 128), filt_h[1].reshape(256, 128)
    prod = jnp.concatenate([s_re * h_re - s_im * h_im, s_re * h_im + s_im * h_re], axis=1).astype(BF16)
    part = jnp.dot(prod, shortb[...], preferred_element_type=F32).reshape(4, 64, 256)
    p_re, p_im = part[:, :, :128], part[:, :, 128:]
    bent = jnp.concatenate(
        [p_re * b_re + p_im * b_im, p_im * b_re - p_re * b_im], axis=0
    ).reshape(512, 128).astype(BF16)
    for peers in planes:
        block = peers[0][0]
        part = jnp.dot(wideb[block], bent, preferred_element_type=F32)
        out3[block] = part.reshape(16, 8, 128).astype(BF16)
        for x2, z2, core2, device in peers:
            s2 = ((z2 >> 2) << 3) | (core2 << 2) | (z2 & 3)
            if peers is planes[-1] and device is peers[-1][-1]:
                in3[freq_id] = out3[block, s2]
            else:
                send(out3.at[block, s2], in3.at[freq_id], 2, device)

    arrived(in3, 63, 2)

    for block in range(4):
        even = in3[pl.ds(8 * block, 8)].astype(F32)
        odd = in3[pl.ds(32 + 8 * block, 8)].astype(F32)
        e_re = jnp.where(low4, even, pltpu.roll(odd, 4, 1))
        e_im = jnp.where(low4, pltpu.roll(even, 4, 1), odd)
        at = pl.ds(8 * block, 8)
        w_re, w_im = twist[0, at], twist[1, at]
        spread = []
        for g in (e_re * w_re + e_im * w_im, e_im * w_re - e_re * w_im):
            u = [jnp.where(low32, g, pltpu.roll(g, 32, 2)), jnp.where(low32, pltpu.roll(g, 96, 2), g)]
            r = [pltpu.roll(a, 64, 2) for a in u]
            spread.append(
                [jnp.where(low64, u[e], r[e]) for e in range(2)]
                + [jnp.where(low64, r[e], u[e]) for e in range(2)]
            )
        for ka in range(4):
            t_re, t_im = turn[0, ka].reshape(8, 8, 128), turn[1, ka].reshape(8, 8, 128)
            g_re, g_im = spread[0][ka], spread[1][ka]
            mixed[block, 0, ka] = (g_re * t_re + g_im * t_im).reshape(64, 128).astype(BF16)
            mixed[block, 1, ka] = (g_im * t_re - g_re * t_im).reshape(64, 128).astype(BF16)
    total = jnp.dot(back[...], mixed[...].reshape(2048, 128), preferred_element_type=F32)
    result = total.reshape(32, 8, 128) * (1.0 / SEQ) + skip[y] * in1[...].astype(F32)
    out4[...] = result.astype(BF16)
    in4[row] = out4[row]

    for y2, zl2, device in row_peers[:-1]:
        send(out4.at[4 * y2 + zl2], in4.at[row], 3, device)

    def sent(buffer, count, n):
        view = buffer.at[pl.ds(0, count)]
        pltpu.make_async_copy(view, view, send_sem.at[n]).wait()

    sent(in1, 31, 0)
    sent(out2, 63, 1)
    sent(in3, 63, 2)

    @pl.when(own)
    def _():
        view = filt_in.at[:, pl.ds(0, 15)]
        pltpu.make_async_copy(view, view, send_sem.at[4]).wait()

    @pl.when(jnp.logical_not(own))
    def _():
        pltpu.make_async_copy(filt_in, filt_in, send_sem.at[4]).wait()

    arrived(in4, 31, 3)
    blocks = in4[...].astype(F32).reshape(8, 4, 8, 128)
    out[...] = jnp.concatenate(regroup([blocks[:, b] for b in range(4)]), axis=1).astype(BF16)
    sent(out4, 31, 3)


def solution(mesh):
    consts = tables()
    hbm, vmem = pl.BlockSpec(memory_space=pl.ANY), pl.BlockSpec(memory_space=pltpu.VMEM)
    like = lambda a, kind: pltpu.VMEM(a.shape, kind)
    kinds = (BF16, BF16, F32, BF16, BF16, F32, BF16, BF16)

    def local(signal, filter_real, filter_imag, skip):
        return pl.pallas_call(
            kernel,
            out_shape=jax.ShapeDtypeStruct(signal.shape, BF16),
            in_specs=[hbm] * 3 + [pl.BlockSpec(memory_space=pltpu.SMEM)] + [hbm] * 8,
            out_specs=vmem,
            scratch_shapes=[
                pltpu.VMEM((8, 32, 128), BF16),
                pltpu.VMEM((8, 4, 8, 128), BF16),
                pltpu.VMEM((32, 8, 128), BF16),
                pltpu.VMEM((64, 8, 128), BF16),
                pltpu.VMEM((64, 8, 128), BF16),
                pltpu.VMEM((4, 16, 8, 128), BF16),
                pltpu.VMEM((64, 8, 128), BF16),
                pltpu.VMEM((32, 8, 128), BF16),
                pltpu.VMEM((32, 8, 128), BF16),
                pltpu.VMEM((2, 16, 16, 128), BF16),
                pltpu.VMEM((2, 256, 128), F32),
                pltpu.VMEM((2, 4, 64, 128), F32),
                pltpu.VMEM((2, 32, 8, 128), F32),
                pltpu.VMEM((4, 2, 4, 64, 128), BF16),
                *[like(a, kind) for a, kind in zip(consts, kinds)],
                pltpu.SemaphoreType.DMA((9,)),
                pltpu.SemaphoreType.DMA((5,)),
                pltpu.SemaphoreType.DMA((5,)),
            ],
            compiler_params=pltpu.CompilerParams(
                collective_id=0, has_side_effects=True, vmem_limit_bytes=56 << 20
            ),
        )(signal, filter_real, filter_imag, skip, *consts)

    block = P(None, "row", "col")
    return jax.shard_map(
        local, mesh=mesh, in_specs=(block, block, block, P()), out_specs=block, check_vma=False
    )
```

```python
import functools

import jax
import jax.numpy as jnp
import numpy as np
from jax import lax
from jax.experimental import pallas as pl
from jax.experimental.pallas import tpu as pltpu
from jax.sharding import PartitionSpec as P

MESH = pl.DeviceIdType.MESH
F32, BF16 = jnp.float32, jnp.bfloat16
N1, N2 = 1024, 2048
SEQ = N1 * N2
VMEM_BYTES = 55142 << 10


def unit(product, modulus):
    angle = 2.0 * np.pi / modulus * (product % modulus)
    return np.cos(angle), np.sin(angle)


def tables():
    g = lambda *dims: np.meshgrid(*[np.arange(n) for n in dims], indexing="ij")
    bl, ka, dl, dh, kb, r, i = g(4, 4, 8, 2, 4, 32, 8)
    k1 = 16 * (8 * bl + dl + 32 * dh) + 4 * ka + kb
    c, s = unit(k1 * (32 * r + i), N1)
    first = np.stack([c, -s], axis=1).reshape(4, 512, 256)
    ka, dl, dh, kb, k, j = g(4, 8, 2, 4, 4, 32)
    c, s = unit((16 * (dl + 32 * dh) + 4 * ka + kb) * 8 * k, N1)
    turn = np.stack([c, -s]).reshape(2, 4, 64, 128)
    c, s = unit(np.outer(np.arange(64), np.arange(64)), 64)
    wide = np.einsum("pqks,bc->pbksqc", np.array([[c, s], [-s, c]]), np.eye(4)).reshape(512, 512)
    ks, ka, j = g(64, 4, 32)
    c, s = unit(j * ks, N2)
    bend = np.stack([c, -s]).reshape(2, 64, 128)
    j, kj0, q = g(32, 2, 16)
    c, s = unit(j * (2 * q + kj0), 32)
    short = np.einsum("pqjhx,ab->pajqhbx", np.array([[c, -s], [s, c]]), np.eye(4)).reshape(256, 256)
    half = lambda a: np.asarray(a, np.float32).astype(BF16)
    full = lambda a: np.asarray(a, np.float32)
    return (
        half(first),
        half(first.reshape(2048, 256).T),
        full(turn),
        half(wide),
        half(wide.T.reshape(2, 4, 8, 8, 512).transpose(1, 0, 2, 3, 4).reshape(4, 128, 512)),
        full(bend),
        half(short),
        half(short.T),
    )


FAR8 = (4, 3, 5, 2, 6, 1, 7, 0)
FAR4 = (2, 1, 3, 0)


def kernel(
    signal, filt_re, filt_im,
    c_first, c_back, c_turn, c_wide, c_wideb, c_bend, c_short, c_shortb,
    out,
    x_in, out1, in1, out2, in2, out3, in3, out4, in4, filt_in, filt_f, filt_h, twist, mixed,
    first, back, turn, wide, wideb, bend, short, shortb,
    load_sem, send_sem, recv_sem,
):
    row, col = lax.axis_index("row"), lax.axis_index("col")
    y, zl = row >> 2, row & 3
    z, xs, core = ((col >> 3) << 2) | zl, (col >> 1) & 3, col & 1
    col_id = 4 * col + zl
    freq_id = 8 * (col >> 1) + 2 * zl + core

    loads = [
        pltpu.make_async_copy(a, b, load_sem.at[n])
        for n, (a, b) in enumerate((
            (signal, x_in), (c_first, first), (c_turn, turn), (c_wide, wide), (c_bend, bend),
            (c_short, short), (c_shortb, shortb), (c_wideb, wideb), (c_back, back),
        ))
    ]
    loads[0].start()

    row_peers = []
    for dy in FAR8:
        for dz in (3, 2, 1, 0):
            y2, zl2 = (y + dy) & 7, (zl + dz) & 3
            row_peers.append((y2, zl2, (4 * y2 + zl2, col)))
    planes = []
    for dx in FAR4:
        planes.append([])
        for dz in FAR8:
            for dc in (1, 0):
                z2, x2, core2 = (z + dz) & 7, (xs + dx) & 3, core ^ dc
                zl2, col2 = z2 & 3, ((z2 >> 2) << 3) | (x2 << 1) | core2
                planes[-1].append((x2, z2, core2, (4 * y + zl2, col2)))
    cols = []
    for dz in (1, 0):
        for dx in FAR4:
            for dc in (1, 0):
                cols.append((col ^ (8 * dz + dc)) & 9 | (((xs + dx) & 3) << 1))

    own = (col >> 1) == y
    barrier = pltpu.get_barrier_semaphore()
    hear = lambda device: pl.semaphore_signal(barrier, inc=1, device_id=device, device_id_type=MESH)
    for col2 in cols[:-1]:
        hear((4 * (col >> 1) + zl, col2))

    @pl.when(jnp.logical_not(own))
    def _():
        hear((4 * (col >> 1) + zl, col))

    for peer in row_peers[:-1]:
        hear(peer[-1])
    for peer in sum(planes, [])[:-1]:
        hear(peer[-1])

    lane = lax.broadcasted_iota(jnp.int32, (8, 128), 1)
    low64, low32 = lane < 64, (lane & 32) == 0
    low4 = lax.broadcasted_iota(jnp.int32, (8, 128), 0) < 4

    def regroup(a):
        u = [[None, None], [None, None]]
        for e in range(2):
            u[0][e] = jnp.where(low64, a[e], pltpu.roll(a[2 + e], 64, 2))
            u[1][e] = jnp.where(low64, pltpu.roll(a[e], 64, 2), a[2 + e])
        v = []
        for b in range(2):
            v.append(jnp.where(low32, u[b][0], pltpu.roll(u[b][1], 32, 2)))
            v.append(jnp.where(low32, pltpu.roll(u[b][0], 96, 2), u[b][1]))
        return v

    for load in loads[1:]:
        load.start()

    loads[0].wait()
    pieces = x_in[...].astype(F32)
    for b, piece in enumerate(regroup([pieces[:, 8 * k : 8 * k + 8, :] for k in range(4)])):
        out1[:, b] = piece.astype(BF16)
    in1[row] = out1[y, zl]

    pl.semaphore_wait(barrier, 31 + 63 + 16 - own.astype(jnp.int32))

    def send(source, target, n, device):
        pltpu.make_async_remote_copy(
            src_ref=source, dst_ref=target, send_sem=send_sem.at[n], recv_sem=recv_sem.at[n],
            device_id=device, device_id_type=MESH,
        ).start()

    for y2, zl2, device in row_peers[:-1]:
        send(out1.at[y2, zl2], in1.at[row], 0, device)

    for dy in FAR8:
        for dc in (1, 0):
            c, h = (y + dy) & 7, core ^ dc
            for n, part in enumerate((filt_re, filt_im)):
                source, target = part.at[c, pl.ds(16 * h, 16)], filt_in.at[n, col]
                if dy or dc:
                    send(source, target, 4, (4 * c + zl, 2 * y + h))
                    continue

                @pl.when(own)
                def _():
                    pltpu.make_async_copy(source, target, recv_sem.at[4]).start()

                @pl.when(jnp.logical_not(own))
                def _():
                    send(source, target, 4, (4 * c + zl, 2 * y + h))

    @pl.loop(0, 32)
    def _(dl):
        sub = lax.broadcasted_iota(jnp.int32, (8, 128), 0)
        k1 = 16 * (dl + 32 * (sub >> 2)) + 4 * (lane >> 5) + (sub & 3)
        n2 = 32 * col_id + (lane & 31)
        angle = (-2.0 * np.pi / SEQ) * (k1 * n2).astype(F32)
        twist[0, dl] = jnp.cos(angle)
        twist[1, dl] = jnp.sin(angle)

    def arrived(buffer, count, n):
        view = buffer.at[pl.ds(0, count)]
        pltpu.make_async_copy(view, view, recv_sem.at[n]).wait()

    for load in loads[1:]:
        load.wait()
    arrived(in1, 31, 0)

    columns = in1[...].astype(F32).reshape(256, 128).astype(BF16)
    for peers in planes:
        block = peers[0][0]
        part = jnp.dot(first[block], columns, preferred_element_type=F32).reshape(2, 4, 8, 8, 128)
        turned = [[], []]
        for ka in range(4):
            t_re, t_im = turn[0, ka].reshape(8, 8, 128), turn[1, ka].reshape(8, 8, 128)
            turned[0].append(part[0, ka] * t_re - part[1, ka] * t_im)
            turned[1].append(part[0, ka] * t_im + part[1, ka] * t_re)
        summed = []
        for v in turned:
            u = [
                jnp.where(low64, v[e], v[2 + e]) + pltpu.roll(jnp.where(low64, v[2 + e], v[e]), 64, 2)
                for e in range(2)
            ]
            summed.append(
                jnp.where(low32, u[0] + pltpu.roll(u[0], 96, 2), u[1] + pltpu.roll(u[1], 32, 2))
            )
        at = pl.ds(8 * block, 8)
        w_re, w_im = twist[0, at], twist[1, at]
        m_re = summed[0] * w_re - summed[1] * w_im
        m_im = summed[0] * w_im + summed[1] * w_re
        out2[pl.ds(8 * block, 8)] = jnp.where(low4, m_re, pltpu.roll(m_im, 4, 1)).astype(BF16)
        out2[pl.ds(32 + 8 * block, 8)] = jnp.where(low4, pltpu.roll(m_re, 4, 1), m_im).astype(BF16)
        for x2, z2, core2, device in peers:
            d2 = ((z2 >> 2) << 5) | (x2 << 3) | ((z2 & 3) << 1) | core2
            if peers is planes[-1] and device is peers[-1][-1]:
                in2[col_id] = out2[d2]
            else:
                send(out2.at[d2], in2.at[col_id], 1, device)

    for n in range(2):
        view = filt_in.at[n]
        if n == 0:
            pltpu.make_async_copy(filt_in, filt_in, recv_sem.at[4]).wait()
        filt_f[n] = filt_in[n].astype(F32).reshape(256, 128)
        for pair in range(2):
            rows = [
                filt_f[n, pl.ds(4 * ka + 2 * pair + e, 16, stride=16), :]
                for e in range(2)
                for ka in range(4)
            ]
            turned = jnp.concatenate(rows, axis=0).T
            upper, lower = turned[:64].reshape(8, 8, 128), turned[64:].reshape(8, 8, 128)
            filt_h[n, 2 * pair] = jnp.where(low64, upper, pltpu.roll(lower, 64, 2)).reshape(64, 128)
            filt_h[n, 2 * pair + 1] = jnp.where(low64, pltpu.roll(upper, 64, 2), lower).reshape(64, 128)

    arrived(in2, 63, 1)

    series = in2[...].astype(F32).reshape(512, 128).astype(BF16)
    part = jnp.dot(wide[...], series, preferred_element_type=F32).reshape(2, 4, 64, 128)
    b_re, b_im = bend[0], bend[1]
    bent = jnp.concatenate(
        [part[0] * b_re - part[1] * b_im, part[0] * b_im + part[1] * b_re], axis=2
    ).reshape(256, 256).astype(BF16)
    spec = jnp.dot(bent, short[...], preferred_element_type=F32)
    s_re, s_im = spec[:, :128], spec[:, 128:]
    h_re, h_im = filt_h[0].reshape(256, 128), filt_h[1].reshape(256, 128)
    prod = jnp.concatenate([s_re * h_re - s_im * h_im, s_re * h_im + s_im * h_re], axis=1).astype(BF16)
    part = jnp.dot(prod, shortb[...], preferred_element_type=F32).reshape(4, 64, 256)
    p_re, p_im = part[:, :, :128], part[:, :, 128:]
    bent = jnp.concatenate(
        [p_re * b_re + p_im * b_im, p_im * b_re - p_re * b_im], axis=0
    ).reshape(512, 128).astype(BF16)
    for peers in planes:
        block = peers[0][0]
        part = jnp.dot(wideb[block], bent, preferred_element_type=F32)
        out3[block] = part.reshape(16, 8, 128).astype(BF16)
        for x2, z2, core2, device in peers:
            s2 = ((z2 >> 2) << 3) | (core2 << 2) | (z2 & 3)
            if peers is planes[-1] and device is peers[-1][-1]:
                in3[freq_id] = out3[block, s2]
            else:
                send(out3.at[block, s2], in3.at[freq_id], 2, device)

    arrived(in3, 63, 2)

    for block in range(4):
        even = in3[pl.ds(8 * block, 8)].astype(F32)
        odd = in3[pl.ds(32 + 8 * block, 8)].astype(F32)
        e_re = jnp.where(low4, even, pltpu.roll(odd, 4, 1))
        e_im = jnp.where(low4, pltpu.roll(even, 4, 1), odd)
        at = pl.ds(8 * block, 8)
        w_re, w_im = twist[0, at], twist[1, at]
        spread = []
        for g in (e_re * w_re + e_im * w_im, e_im * w_re - e_re * w_im):
            u = [jnp.where(low32, g, pltpu.roll(g, 32, 2)), jnp.where(low32, pltpu.roll(g, 96, 2), g)]
            r = [pltpu.roll(a, 64, 2) for a in u]
            spread.append(
                [jnp.where(low64, u[e], r[e]) for e in range(2)]
                + [jnp.where(low64, r[e], u[e]) for e in range(2)]
            )
        for ka in range(4):
            t_re, t_im = turn[0, ka].reshape(8, 8, 128), turn[1, ka].reshape(8, 8, 128)
            g_re, g_im = spread[0][ka], spread[1][ka]
            mixed[block, 0, ka] = (g_re * t_re + g_im * t_im).reshape(64, 128).astype(BF16)
            mixed[block, 1, ka] = (g_im * t_re - g_re * t_im).reshape(64, 128).astype(BF16)
    total = jnp.dot(back[...], mixed[...].reshape(2048, 128), preferred_element_type=F32)
    result = total.reshape(32, 8, 128) * (1.0 / SEQ)
    out4[...] = result.astype(BF16)
    in4[row] = out4[row]

    for y2, zl2, device in row_peers[:-1]:
        send(out4.at[4 * y2 + zl2], in4.at[row], 3, device)

    def sent(buffer, count, n):
        view = buffer.at[pl.ds(0, count)]
        pltpu.make_async_copy(view, view, send_sem.at[n]).wait()

    sent(in1, 31, 0)
    sent(out2, 63, 1)
    sent(in3, 63, 2)

    @pl.when(own)
    def _():
        view = filt_in.at[:, pl.ds(0, 15)]
        pltpu.make_async_copy(view, view, send_sem.at[4]).wait()

    @pl.when(jnp.logical_not(own))
    def _():
        pltpu.make_async_copy(filt_in, filt_in, send_sem.at[4]).wait()

    arrived(in4, 31, 3)
    blocks = in4[...].astype(F32).reshape(8, 4, 8, 128)
    out[...] = jnp.concatenate(regroup([blocks[:, b] for b in range(4)]), axis=1).astype(BF16)
    sent(out4, 31, 3)


def solution(mesh):
    consts = tables()
    hbm, vmem = pl.BlockSpec(memory_space=pl.ANY), pl.BlockSpec(memory_space=pltpu.VMEM)
    like = lambda a, kind: pltpu.VMEM(a.shape, kind)
    kinds = (BF16, BF16, F32, BF16, BF16, F32, BF16, BF16)

    def local(signal, filter_real, filter_imag, skip):
        conv = pl.pallas_call(
            kernel,
            out_shape=jax.ShapeDtypeStruct(signal.shape, BF16),
            in_specs=[hbm] * 11,
            out_specs=vmem,
            scratch_shapes=[
                pltpu.VMEM((8, 32, 128), BF16),
                pltpu.VMEM((8, 4, 8, 128), BF16),
                pltpu.VMEM((32, 8, 128), BF16),
                pltpu.VMEM((64, 8, 128), BF16),
                pltpu.VMEM((64, 8, 128), BF16),
                pltpu.VMEM((4, 16, 8, 128), BF16),
                pltpu.VMEM((64, 8, 128), BF16),
                pltpu.VMEM((32, 8, 128), BF16),
                pltpu.VMEM((32, 8, 128), BF16),
                pltpu.VMEM((2, 16, 16, 128), BF16),
                pltpu.VMEM((2, 256, 128), F32),
                pltpu.VMEM((2, 4, 64, 128), F32),
                pltpu.VMEM((2, 32, 8, 128), F32),
                pltpu.VMEM((4, 2, 4, 64, 128), BF16),
                *[like(a, kind) for a, kind in zip(consts, kinds)],
                pltpu.SemaphoreType.DMA((9,)),
                pltpu.SemaphoreType.DMA((5,)),
                pltpu.SemaphoreType.DMA((5,)),
            ],
            compiler_params=pltpu.CompilerParams(
                collective_id=0, has_side_effects=True, vmem_limit_bytes=VMEM_BYTES
            ),
        )(signal, filter_real, filter_imag, *consts)
        return (conv.astype(F32) + skip[:, None, None] * signal.astype(F32)).astype(BF16)

    block = P(None, "row", "col")
    return jax.shard_map(
        local, mesh=mesh, in_specs=(block, block, block, P()), out_specs=block, check_vma=False
    )
```

```python
import functools

import jax
import jax.numpy as jnp
import numpy as np
from jax import lax
from jax.experimental import pallas as pl
from jax.experimental.pallas import tpu as pltpu
from jax.sharding import PartitionSpec as P

MESH = pl.DeviceIdType.MESH
F32, BF16 = jnp.float32, jnp.bfloat16
N1, N2 = 1024, 2048
SEQ = N1 * N2
VMEM_BYTES = 55142 << 10


def unit(product, modulus):
    angle = 2.0 * np.pi / modulus * (product % modulus)
    return np.cos(angle), np.sin(angle)


def tables():
    g = lambda *dims: np.meshgrid(*[np.arange(n) for n in dims], indexing="ij")
    bl, ka, dl, dh, kb, r, i = g(4, 4, 8, 2, 4, 32, 8)
    k1 = 16 * (8 * bl + dl + 32 * dh) + 4 * ka + kb
    c, s = unit(k1 * (32 * r + i), N1)
    first = np.stack([c, -s], axis=1).reshape(4, 512, 256)
    ka, dl, dh, kb, k, j = g(4, 8, 2, 4, 4, 32)
    c, s = unit((16 * (dl + 32 * dh) + 4 * ka + kb) * 8 * k, N1)
    turn = np.stack([c, -s]).reshape(2, 4, 64, 128)
    c, s = unit(np.outer(np.arange(64), np.arange(64)), 64)
    wide = np.einsum("pqks,bc->pbksqc", np.array([[c, s], [-s, c]]), np.eye(4)).reshape(512, 512)
    ks, ka, j = g(64, 4, 32)
    c, s = unit(j * ks, N2)
    bend = np.stack([c, -s]).reshape(2, 64, 128)
    j, kj0, q = g(32, 2, 16)
    c, s = unit(j * (2 * q + kj0), 32)
    short = np.einsum("pqjhx,ab->pajqhbx", np.array([[c, -s], [s, c]]), np.eye(4)).reshape(256, 256)
    half = lambda a: np.asarray(a, np.float32).astype(BF16)
    full = lambda a: np.asarray(a, np.float32)
    return (
        half(first),
        half(first.reshape(2048, 256).T),
        full(turn),
        half(wide),
        half(wide.T.reshape(2, 4, 8, 8, 512).transpose(1, 0, 2, 3, 4).reshape(4, 128, 512)),
        full(bend),
        half(short),
        half(short.T),
    )


FAR8 = (4, 3, 5, 2, 6, 1, 7, 0)
FAR4 = (2, 1, 3, 0)


def kernel(
    signal, filt_re, filt_im,
    c_first, c_back, c_turn, c_wide, c_wideb, c_bend, c_short, c_shortb,
    out,
    x_in, out1, in1, out2, in2, out3, in3, out4, in4, filt_in, filt_f, filt_h, twist, mixed,
    first, back, turn, wide, wideb, bend, short, shortb,
    load_sem, send_sem, recv_sem,
):
    row, col = lax.axis_index("row"), lax.axis_index("col")
    y, zl = row >> 2, row & 3
    z, xs, core = ((col >> 3) << 2) | zl, (col >> 1) & 3, col & 1
    col_id = 4 * col + zl
    half = zl ^ 2
    freq_id = 8 * (col >> 1) + 2 * half + core

    loads = [
        pltpu.make_async_copy(a, b, load_sem.at[n])
        for n, (a, b) in enumerate((
            (signal, x_in), (c_first, first), (c_turn, turn), (c_wide, wide), (c_bend, bend),
            (c_short, short), (c_shortb, shortb), (c_wideb, wideb), (c_back, back),
        ))
    ]
    loads[0].start()

    row_peers = []
    for dy in FAR8:
        for dz in (3, 2, 1, 0):
            y2, zl2 = (y + dy) & 7, (zl + dz) & 3
            row_peers.append((y2, zl2, (4 * y2 + zl2, col)))
    planes = []
    for dx in FAR4:
        planes.append([])
        for dz in FAR8:
            for dc in (1, 0):
                z2, x2, core2 = (z + dz) & 7, (xs + dx) & 3, core ^ dc
                zl2, col2 = z2 & 3, ((z2 >> 2) << 3) | (x2 << 1) | core2
                planes[-1].append((x2, z2, core2, (4 * y + zl2, col2)))
    cols = []
    for dz in (1, 0):
        for dx in FAR4:
            for dc in (1, 0):
                cols.append((col ^ (8 * dz + dc)) & 9 | (((xs + dx) & 3) << 1))

    barrier = pltpu.get_barrier_semaphore()
    hear = lambda device: pl.semaphore_signal(barrier, inc=1, device_id=device, device_id_type=MESH)
    for col2 in cols:
        hear((4 * (col >> 1) + half, col2))
    for peer in row_peers[:-1]:
        hear(peer[-1])
    for peer in sum(planes, [])[:-1]:
        hear(peer[-1])

    lane = lax.broadcasted_iota(jnp.int32, (8, 128), 1)
    low64, low32 = lane < 64, (lane & 32) == 0
    low4 = lax.broadcasted_iota(jnp.int32, (8, 128), 0) < 4

    def regroup(a):
        u = [[None, None], [None, None]]
        for e in range(2):
            u[0][e] = jnp.where(low64, a[e], pltpu.roll(a[2 + e], 64, 2))
            u[1][e] = jnp.where(low64, pltpu.roll(a[e], 64, 2), a[2 + e])
        v = []
        for b in range(2):
            v.append(jnp.where(low32, u[b][0], pltpu.roll(u[b][1], 32, 2)))
            v.append(jnp.where(low32, pltpu.roll(u[b][0], 96, 2), u[b][1]))
        return v

    for load in loads[1:]:
        load.start()

    loads[0].wait()
    pieces = x_in[...].astype(F32)
    for b, piece in enumerate(regroup([pieces[:, 8 * k : 8 * k + 8, :] for k in range(4)])):
        out1[:, b] = piece.astype(BF16)
    in1[row] = out1[y, zl]

    pl.semaphore_wait(barrier, 31 + 63 + 16)

    def send(source, target, n, device):
        pltpu.make_async_remote_copy(
            src_ref=source, dst_ref=target, send_sem=send_sem.at[n], recv_sem=recv_sem.at[n],
            device_id=device, device_id_type=MESH,
        ).start()

    for y2, zl2, device in row_peers[:-1]:
        send(out1.at[y2, zl2], in1.at[row], 0, device)

    for dy in FAR8:
        for dc in (1, 0):
            c, h = (y + dy) & 7, core ^ dc
            for n, part in enumerate((filt_re, filt_im)):
                source, target = part.at[c, pl.ds(16 * h, 16)], filt_in.at[n, col]
                send(source, target, 4, (4 * c + half, 2 * y + h))

    @pl.loop(0, 32)
    def _(dl):
        sub = lax.broadcasted_iota(jnp.int32, (8, 128), 0)
        k1 = 16 * (dl + 32 * (sub >> 2)) + 4 * (lane >> 5) + (sub & 3)
        n2 = 32 * col_id + (lane & 31)
        angle = (-2.0 * np.pi / SEQ) * (k1 * n2).astype(F32)
        twist[0, dl] = jnp.cos(angle)
        twist[1, dl] = jnp.sin(angle)

    def arrived(buffer, count, n):
        view = buffer.at[pl.ds(0, count)]
        pltpu.make_async_copy(view, view, recv_sem.at[n]).wait()

    for load in loads[1:]:
        load.wait()
    arrived(in1, 31, 0)

    columns = in1[...].astype(F32).reshape(256, 128).astype(BF16)
    for peers in planes:
        block = peers[0][0]
        part = jnp.dot(first[block], columns, preferred_element_type=F32).reshape(2, 4, 8, 8, 128)
        turned = [[], []]
        for ka in range(4):
            t_re, t_im = turn[0, ka].reshape(8, 8, 128), turn[1, ka].reshape(8, 8, 128)
            turned[0].append(part[0, ka] * t_re - part[1, ka] * t_im)
            turned[1].append(part[0, ka] * t_im + part[1, ka] * t_re)
        summed = []
        for v in turned:
            u = [
                jnp.where(low64, v[e], v[2 + e]) + pltpu.roll(jnp.where(low64, v[2 + e], v[e]), 64, 2)
                for e in range(2)
            ]
            summed.append(
                jnp.where(low32, u[0] + pltpu.roll(u[0], 96, 2), u[1] + pltpu.roll(u[1], 32, 2))
            )
        at = pl.ds(8 * block, 8)
        w_re, w_im = twist[0, at], twist[1, at]
        m_re = summed[0] * w_re - summed[1] * w_im
        m_im = summed[0] * w_im + summed[1] * w_re
        out2[pl.ds(8 * block, 8)] = jnp.where(low4, m_re, pltpu.roll(m_im, 4, 1)).astype(BF16)
        out2[pl.ds(32 + 8 * block, 8)] = jnp.where(low4, pltpu.roll(m_re, 4, 1), m_im).astype(BF16)
        for x2, z2, core2, device in peers:
            d2 = ((z2 >> 2) << 5) | (x2 << 3) | (((z2 & 3) ^ 2) << 1) | core2
            if peers is planes[-1] and device is peers[-1][-1]:
                in2[col_id] = out2[d2]
            else:
                send(out2.at[d2], in2.at[col_id], 1, device)

    for n in range(2):
        view = filt_in.at[n]
        if n == 0:
            pltpu.make_async_copy(filt_in, filt_in, recv_sem.at[4]).wait()
        filt_f[n] = filt_in[n].astype(F32).reshape(256, 128)
        for pair in range(2):
            rows = [
                filt_f[n, pl.ds(4 * ka + 2 * pair + e, 16, stride=16), :]
                for e in range(2)
                for ka in range(4)
            ]
            turned = jnp.concatenate(rows, axis=0).T
            upper, lower = turned[:64].reshape(8, 8, 128), turned[64:].reshape(8, 8, 128)
            filt_h[n, 2 * pair] = jnp.where(low64, upper, pltpu.roll(lower, 64, 2)).reshape(64, 128)
            filt_h[n, 2 * pair + 1] = jnp.where(low64, pltpu.roll(upper, 64, 2), lower).reshape(64, 128)

    arrived(in2, 63, 1)

    series = in2[...].astype(F32).reshape(512, 128).astype(BF16)
    part = jnp.dot(wide[...], series, preferred_element_type=F32).reshape(2, 4, 64, 128)
    b_re, b_im = bend[0], bend[1]
    bent = jnp.concatenate(
        [part[0] * b_re - part[1] * b_im, part[0] * b_im + part[1] * b_re], axis=2
    ).reshape(256, 256).astype(BF16)
    spec = jnp.dot(bent, short[...], preferred_element_type=F32)
    s_re, s_im = spec[:, :128], spec[:, 128:]
    h_re, h_im = filt_h[0].reshape(256, 128), filt_h[1].reshape(256, 128)
    prod = jnp.concatenate([s_re * h_re - s_im * h_im, s_re * h_im + s_im * h_re], axis=1).astype(BF16)
    part = jnp.dot(prod, shortb[...], preferred_element_type=F32).reshape(4, 64, 256)
    p_re, p_im = part[:, :, :128], part[:, :, 128:]
    bent = jnp.concatenate(
        [p_re * b_re + p_im * b_im, p_im * b_re - p_re * b_im], axis=0
    ).reshape(512, 128).astype(BF16)
    for peers in planes:
        block = peers[0][0]
        part = jnp.dot(wideb[block], bent, preferred_element_type=F32)
        out3[block] = part.reshape(16, 8, 128).astype(BF16)
        for x2, z2, core2, device in peers:
            s2 = ((z2 >> 2) << 3) | (core2 << 2) | (z2 & 3)
            if peers is planes[-1] and device is peers[-1][-1]:
                in3[freq_id] = out3[block, s2]
            else:
                send(out3.at[block, s2], in3.at[freq_id], 2, device)

    arrived(in3, 63, 2)

    for block in range(4):
        even = in3[pl.ds(8 * block, 8)].astype(F32)
        odd = in3[pl.ds(32 + 8 * block, 8)].astype(F32)
        e_re = jnp.where(low4, even, pltpu.roll(odd, 4, 1))
        e_im = jnp.where(low4, pltpu.roll(even, 4, 1), odd)
        at = pl.ds(8 * block, 8)
        w_re, w_im = twist[0, at], twist[1, at]
        spread = []
        for g in (e_re * w_re + e_im * w_im, e_im * w_re - e_re * w_im):
            u = [jnp.where(low32, g, pltpu.roll(g, 32, 2)), jnp.where(low32, pltpu.roll(g, 96, 2), g)]
            r = [pltpu.roll(a, 64, 2) for a in u]
            spread.append(
                [jnp.where(low64, u[e], r[e]) for e in range(2)]
                + [jnp.where(low64, r[e], u[e]) for e in range(2)]
            )
        for ka in range(4):
            t_re, t_im = turn[0, ka].reshape(8, 8, 128), turn[1, ka].reshape(8, 8, 128)
            g_re, g_im = spread[0][ka], spread[1][ka]
            mixed[block, 0, ka] = (g_re * t_re + g_im * t_im).reshape(64, 128).astype(BF16)
            mixed[block, 1, ka] = (g_im * t_re - g_re * t_im).reshape(64, 128).astype(BF16)
    total = jnp.dot(back[...], mixed[...].reshape(2048, 128), preferred_element_type=F32)
    result = total.reshape(32, 8, 128) * (1.0 / SEQ)
    out4[...] = result.astype(BF16)
    in4[row] = out4[row]

    for y2, zl2, device in row_peers[:-1]:
        send(out4.at[4 * y2 + zl2], in4.at[row], 3, device)

    def sent(buffer, count, n):
        view = buffer.at[pl.ds(0, count)]
        pltpu.make_async_copy(view, view, send_sem.at[n]).wait()

    sent(in1, 31, 0)
    sent(out2, 63, 1)
    sent(in3, 63, 2)

    pltpu.make_async_copy(filt_in, filt_in, send_sem.at[4]).wait()
    arrived(in4, 31, 3)
    blocks = in4[...].astype(F32).reshape(8, 4, 8, 128)
    out[...] = jnp.concatenate(regroup([blocks[:, b] for b in range(4)]), axis=1).astype(BF16)
    sent(out4, 31, 3)


def solution(mesh):
    consts = tables()
    hbm, vmem = pl.BlockSpec(memory_space=pl.ANY), pl.BlockSpec(memory_space=pltpu.VMEM)
    like = lambda a, kind: pltpu.VMEM(a.shape, kind)
    kinds = (BF16, BF16, F32, BF16, BF16, F32, BF16, BF16)

    def local(signal, filter_real, filter_imag, skip):
        conv = pl.pallas_call(
            kernel,
            out_shape=jax.ShapeDtypeStruct(signal.shape, BF16),
            in_specs=[hbm] * 11,
            out_specs=vmem,
            scratch_shapes=[
                pltpu.VMEM((8, 32, 128), BF16),
                pltpu.VMEM((8, 4, 8, 128), BF16),
                pltpu.VMEM((32, 8, 128), BF16),
                pltpu.VMEM((64, 8, 128), BF16),
                pltpu.VMEM((64, 8, 128), BF16),
                pltpu.VMEM((4, 16, 8, 128), BF16),
                pltpu.VMEM((64, 8, 128), BF16),
                pltpu.VMEM((32, 8, 128), BF16),
                pltpu.VMEM((32, 8, 128), BF16),
                pltpu.VMEM((2, 16, 16, 128), BF16),
                pltpu.VMEM((2, 256, 128), F32),
                pltpu.VMEM((2, 4, 64, 128), F32),
                pltpu.VMEM((2, 32, 8, 128), F32),
                pltpu.VMEM((4, 2, 4, 64, 128), BF16),
                *[like(a, kind) for a, kind in zip(consts, kinds)],
                pltpu.SemaphoreType.DMA((9,)),
                pltpu.SemaphoreType.DMA((5,)),
                pltpu.SemaphoreType.DMA((5,)),
            ],
            compiler_params=pltpu.CompilerParams(
                collective_id=0, has_side_effects=True, vmem_limit_bytes=VMEM_BYTES
            ),
        )(signal, filter_real, filter_imag, *consts)
        return (conv.astype(F32) + skip[:, None, None] * signal.astype(F32)).astype(BF16)

    block = P(None, "row", "col")
    return jax.shard_map(
        local, mesh=mesh, in_specs=(block, block, block, P()), out_specs=block, check_vma=False
    )
```
